256 devices in a mesh: row: 64 (over y_hi, z, x), col: 4 (over y_lo, core).
Axes of the slice: x: 4, y: 4 (y_hi: 2, y_lo: 2; y = y_hi * 2 + y_lo), z: 8, core: 2. Of those that a mesh axis runs over, the one named last changes fastest.
Arguments:
- diagonal_inverses: bfloat16 [192, 2048, 2048], P('row', 'col'), may hold values from -0.125 to 0.125
- column_basis: bfloat16 [192, 2048, 256], P('row', 'col'), may hold values from -6 to 6
- row_basis: bfloat16 [192, 2048, 256], P('row', 'col'), may hold values from -0.125 to 0.125
- transfer: float32 [192, 256, 256], P('row', 'col'), may hold values from -0.375 to 0.375
- coupling: float32 [192, 256, 256], P('row', 'col'), may hold values from -6 to 6
- ranks: int32 [192], P('row'), may hold values from 128 to 256, as said below
Outputs:
- merged: float32 [192, 256, 256], P('row', 'col')
- parent_skeleton: float32 [192, 256, 256], P('row', 'col')
The draws below stay inside these ranges and needn't reach their ends.
Inputs may be any that keep to these rules, and one draw needn't show every extreme that they name: `ranks`: each rank is 128 or 256; both occur in every draw.
All inputs are finite; a program needn't handle non-finite values.
Results may differ from the reference program's by a relative error of at most 0.0021.
Values may be sent and summed in bfloat16 or wider, within the bound.
No kernel may reach another device: no remote copies, remote signals or barrier semaphores. Data moves between devices by JAX's collectives and lax.ppermute only.
A program may use at most 64 MiB of HBM per device.

```python
import jax
import jax.numpy as jnp
from jax import lax

M = 2048
R = 256
NODE_DEV = 3
BIT = 2
NODES = 192


def draw_ranks(key, part):
    picked = jax.random.randint(key, (NODES,), 1, 3)
    picked = picked.at[0].set(2).at[1].set(1)
    return (picked * (R // 2)).astype(jnp.int32)


def block_levels(key, extent, shards, smallest, top_value):
    def one(axis_at, shards_of):
        steps = jax.random.uniform(jax.random.fold_in(jax.random.fold_in(key, 6), axis_at), (shards_of,), jnp.float32, smallest / len(shards), top_value / len(shards))
        return jnp.repeat(jnp.exp(steps), extent[axis_at] // shards_of).reshape((-1,) + (1,) * (len(extent) - axis_at - 1))

    loudness = one(*shards[0])
    for cut in shards[1:]:
        loudness = loudness * one(*cut)
    return loudness


def normal_values(key, shape, width, most, split=(), kind=jnp.bfloat16):
    values = jax.random.normal(key, shape, jnp.float32) * width
    if len(split) > 0:
        values = block_levels(key, shape, split, -0.22, 0.18) * values
    return jnp.clip(values, min=-most, max=most).astype(kind)


def setup_inputs(seed: int = 0) -> dict:
    keys = jax.random.split(jax.random.key(seed), 7)
    return {
        "diagonal_inverses": normal_values(keys[0], (NODES, M, M), M ** -0.5, 0.125, ((0, 64), (1, 4))),
        "column_basis": normal_values(keys[1], (NODES, M, R), 1.0, 6.0, ((0, 64), (1, 4))),
        "row_basis": normal_values(keys[2], (NODES, M, R), M ** -0.5, 0.125, ((0, 64), (1, 4))),
        "transfer": normal_values(keys[3], (NODES, R, R), R ** -0.5, 0.375, ((0, 64), (1, 4)), jnp.float32),
        "coupling": normal_values(keys[4], (NODES, R, R), 1.0, 6.0, ((0, 64), (1, 4)), jnp.float32),
        "ranks": draw_ranks(jax.random.fold_in(keys[6], 71), 0),
    }


def leaf_skeleton(items):
    block_entry, left_factor_basis, right_factor_basis, live_cols = items
    left_factor_basis = jnp.where(live_cols[None, :], left_factor_basis, jnp.zeros_like(left_factor_basis))
    right_factor_basis = jnp.where(live_cols[None, :], right_factor_basis, jnp.zeros_like(right_factor_basis))
    eliminated_part = jnp.dot(block_entry, left_factor_basis, preferred_element_type=jnp.float32).astype(jnp.bfloat16)
    return jnp.dot(right_factor_basis.T, eliminated_part, preferred_element_type=jnp.float32)


def reference(diagonal_inverses, column_basis, row_basis, transfer, coupling, ranks):
    node_count = transfer.shape[0]
    rank_width = transfer.shape[1]
    live_cols = jnp.arange(rank_width, dtype=jnp.int32)[None, :] < ranks[:, None]
    skeleton = lax.map(leaf_skeleton, (diagonal_inverses, column_basis, row_basis, live_cols))
    masked = transfer * live_cols[:, :, None].astype(jnp.float32)
    node_ids = jnp.arange(node_count, dtype=jnp.int32)
    sibling = jnp.bitwise_xor(node_ids // NODE_DEV, 2 ** BIT) * NODE_DEV + node_ids % NODE_DEV
    masked_sib = masked[sibling]
    highest = lax.Precision.HIGHEST
    merged = jnp.einsum('nij,njk->nik', skeleton, masked, precision=highest)
    merged = merged + jnp.einsum('nij,njk->nik', coupling, masked_sib, precision=highest)
    parent = jnp.einsum('nji,njk->nik', masked, merged, precision=highest)
    parent = parent + jnp.einsum('nji,njk->nik', masked_sib, merged[sibling], precision=highest)
    return merged, parent
```

```python
import functools

import jax
import jax.numpy as jnp
from jax import lax
from jax.experimental import pallas as pl
from jax.experimental.pallas import tpu as pltpu
from jax.sharding import PartitionSpec as P

BIT = 2
F32 = jnp.float32
BF16 = jnp.bfloat16
HIGH = lax.Precision.HIGHEST
WIDTH = 2.0**17
CORE = [(0, 1), (1, 0), (2, 3), (3, 2)]
CHIP = [(0, 2), (2, 0), (1, 3), (3, 1)]


def siblings():
    count = lax.axis_size("row")
    return [(low, low ^ 1 << BIT) for low in range(count)]


def to_core(block):
    return lax.ppermute(block, "col", CORE)


def to_chip(block):
    return lax.ppermute(block, "col", CHIP)


def to_sibling(block):
    return lax.ppermute(block, "row", siblings())


def params(mib):
    return pltpu.CompilerParams(vmem_limit_bytes=mib << 20)


def dot(a, b, dims=((1,), (0,)), precision=None):
    return lax.dot_general(a, b, (dims, ((), ())), precision=precision, preferred_element_type=F32)


def eliminate_kernel(info, d, own, core, chip, cross, right, out):
    depth = own.shape[1]
    q = info[0]

    def term(k, part):
        start = pl.multiple_of((q ^ k) * depth, depth)
        return dot(d[0, :, pl.ds(start, depth)], part)

    elim = term(0, own[0]) + term(1, core[0]) + term(2, chip[...]) + term(3, cross[...])
    piece = dot(right[0], elim.astype(BF16), ((0,), (0,)))

    @pl.when(pl.program_id(0) == 0)
    def _():
        out[...] = piece

    @pl.when(pl.program_id(0) != 0)
    def _():
        out[...] += piece


def eliminate(n, info, d, own, core, chip, cross, right, steps=2):
    rows, depth, width = d.shape[1], own.shape[1], own.shape[2]
    tile = rows // steps
    whole = pl.BlockSpec((1, depth, width), lambda i, s: (n, 0, 0))
    flat = pl.BlockSpec((depth, width), lambda i, s: (0, 0))
    return pl.pallas_call(
        eliminate_kernel,
        grid_spec=pltpu.PrefetchScalarGridSpec(
            num_scalar_prefetch=1,
            grid=(steps,),
            in_specs=[
                pl.BlockSpec((1, tile, d.shape[2]), lambda i, s: (n, i, 0)),
                whole,
                whole,
                flat,
                flat,
                pl.BlockSpec((1, tile, width), lambda i, s: (n, i, 0)),
            ],
            out_specs=pl.BlockSpec((width, width), lambda i, s: (0, 0)),
        ),
        out_shape=jax.ShapeDtypeStruct((width, width), F32),
        compiler_params=params(16),
        cost_estimate=pl.CostEstimate(flops=2 * rows * width * (d.shape[2] + width), bytes_accessed=4 << 20, transcendentals=0),
        name=f"eliminate{n}",
    )(info, d, own, core, chip, cross, right)


def couple_kernel(info, blocks, c_own, c_core, m_out, cm_out, sib, c_all):
    q = info[0]
    part = blocks.shape[3]
    for k in range(4):
        rows = pl.ds(pl.multiple_of((q ^ k) * part, part), part)
        m_out[0, rows, :] = blocks[k, 0, 0]
        sib[rows, :] = blocks[k, 1, 0]
    half = q & 1
    c_all[pl.ds(pl.multiple_of(half * part, part), part), :] = c_own[0]
    c_all[pl.ds(pl.multiple_of((1 - half) * part, part), part), :] = c_core[0]
    cm_out[0] = dot(c_all[...], sib[...], precision=HIGH)


def couple(info, blocks, c_own, c_core):
    nodes, part, width = c_own.shape
    one = pl.BlockSpec((1, part, width), lambda n, s: (n, 0, 0))
    return pl.pallas_call(
        couple_kernel,
        grid_spec=pltpu.PrefetchScalarGridSpec(
            num_scalar_prefetch=1,
            grid=(nodes,),
            in_specs=[pl.BlockSpec((4, 2, 1, part, width), lambda n, s: (0, 0, n, 0, 0)), one, one],
            out_specs=[
                pl.BlockSpec((1, width, width), lambda n, s: (n, 0, 0)),
                pl.BlockSpec((1, 2 * part, width), lambda n, s: (n, 0, 0)),
            ],
            scratch_shapes=[pltpu.VMEM((width, width), F32), pltpu.VMEM((2 * part, width), F32)],
        ),
        out_shape=[
            jax.ShapeDtypeStruct((nodes, width, width), F32),
            jax.ShapeDtypeStruct((nodes, 2 * part, width), F32),
        ],
        compiler_params=params(16),
        cost_estimate=pl.CostEstimate(flops=12 * nodes * 2 * part * width * width, bytes_accessed=4 << 20, transcendentals=0),
        name="couple",
    )(info, blocks, c_own, c_core)


def merge_kernel(n, info, s_own, s_core, m, cm, t_own, p_own, send, t_all, p_all):
    q = info[0]
    rank = info[1 + n]
    part = t_own.shape[0]
    width = t_own.shape[1]
    row = lax.broadcasted_iota(jnp.int32, (width, width), 0)
    col = lax.broadcasted_iota(jnp.int32, (width, width), 1)
    s = jnp.where((row < rank) & (col < rank), s_own[...] + s_core[...], 0.0)
    t_all[...] = dot(s, m[0], precision=HIGH)
    t_all[pl.ds(pl.multiple_of((q >> 1) * (2 * part), 2 * part), 2 * part), :] += cm[0]
    p_all[...] = dot(m[0], t_all[...], ((0,), (0,)), precision=HIGH)
    mine = pl.ds(pl.multiple_of(q * part, part), part)
    other = pl.ds(pl.multiple_of((q ^ 2) * part, part), part)
    t_own[...] = t_all[mine, :]
    p_own[...] = p_all[mine, :]
    send[0:part, :] = t_all[other, :].astype(BF16)
    send[part : 2 * part, :] = p_all[other, :].astype(BF16)


def merge(n, info, s_own, s_core, m, cm):
    width = m.shape[2]
    part = cm.shape[1] // 2
    flat = pl.BlockSpec((width, width), lambda i, s: (0, 0))
    piece = pl.BlockSpec((part, width), lambda i, s: (0, 0))
    return pl.pallas_call(
        functools.partial(merge_kernel, n),
        grid_spec=pltpu.PrefetchScalarGridSpec(
            num_scalar_prefetch=1,
            grid=(1,),
            in_specs=[
                flat,
                flat,
                pl.BlockSpec((1, width, width), lambda i, s: (n, 0, 0)),
                pl.BlockSpec((1, 2 * part, width), lambda i, s: (n, 0, 0)),
            ],
            out_specs=[piece, piece, pl.BlockSpec((2 * part, width), lambda i, s: (0, 0))],
            scratch_shapes=[pltpu.VMEM((width, width), F32), pltpu.VMEM((width, width), F32)],
        ),
        out_shape=[
            jax.ShapeDtypeStruct((part, width), F32),
            jax.ShapeDtypeStruct((part, width), F32),
            jax.ShapeDtypeStruct((2 * part, width), BF16),
        ],
        compiler_params=params(16),
        cost_estimate=pl.CostEstimate(flops=24 * width**3, bytes_accessed=1 << 20, transcendentals=0),
        name=f"merge{n}",
    )(info, s_own, s_core, m, cm)


def shards(diagonal_inverses, column_basis, row_basis, transfer, coupling, ranks):
    nodes, part, width = transfer.shape
    q = lax.axis_index("col").astype(jnp.int32)
    info = jnp.concatenate([q[None], ranks.astype(jnp.int32)])

    chip_left = [to_chip(column_basis[n]) for n in range(nodes)]
    core_left = to_core(column_basis)
    cross_left = [to_core(block) for block in chip_left]

    rows = q * part + jnp.arange(part, dtype=jnp.int32)
    masked = jnp.where((rows[None, :] < ranks[:, None])[:, :, None], transfer, 0.0)
    m_own = (masked * WIDTH).astype(jnp.float16)
    m_pair = jnp.stack([m_own, to_chip(m_own)])
    m_sib = to_sibling(m_pair)
    m_mine = jnp.stack([m_pair, m_sib], 1)
    m_core = to_core(m_mine)
    blocks = jnp.stack([m_mine[0], m_core[0], m_mine[1], m_core[1]]).astype(F32) * (1 / WIDTH)
    whole, coupled = couple(info, blocks, coupling, to_core(coupling))

    merged, parent = [], []
    for n in range(nodes):
        s = eliminate(n, info, diagonal_inverses, column_basis, core_left, chip_left[n], cross_left[n], row_basis)
        t_own, p_own, send = merge(n, info, s, to_core(s), whole, coupled)
        got = to_chip(send).astype(F32)
        merged.append(t_own + got[:part])
        p_pair = p_own + got[part:]
        parent.append(p_pair + to_sibling(p_pair))
    return jnp.stack(merged), jnp.stack(parent)


def solution(mesh):
    block = P("row", "col", None)
    return jax.shard_map(
        shards,
        mesh=mesh,
        in_specs=(block, block, block, block, block, P("row")),
        out_specs=(block, block),
        check_vma=False,
    )
```

```python
import functools

import jax
import jax.numpy as jnp
from jax import lax
from jax.experimental import pallas as pl
from jax.experimental.pallas import tpu as pltpu
from jax.sharding import PartitionSpec as P

BIT = 2
F32 = jnp.float32
BF16 = jnp.bfloat16
F16 = jnp.float16
SCALE = 2.0**17
CORE = [(0, 1), (1, 0), (2, 3), (3, 2)]
CHIP = [(0, 2), (2, 0), (1, 3), (3, 1)]
VMEM = pl.BlockSpec(memory_space=pltpu.VMEM)
SMEM = pl.BlockSpec(memory_space=pltpu.SMEM)


def to_core(block):
    return lax.ppermute(block, "col", CORE)


def to_chip(block):
    return lax.ppermute(block, "col", CHIP)


def to_sibling(block):
    return lax.ppermute(block, "row", [(n, n ^ 1 << BIT) for n in range(lax.axis_size("row"))])


def after(block, *earlier):
    return lax.optimization_barrier((block, *earlier))[0]


def dot(a, b):
    return lax.dot_general(a, b, (((1,), (0,)), ((), ())), preferred_element_type=F32)


def band(index, size):
    return pl.ds(pl.multiple_of(index * size, size), size)


def split(x):
    high = x.astype(BF16)
    return high, (x - high.astype(F32)).astype(BF16)


def across(x):
    high, low = split(x)
    return jnp.concatenate([high, high, low], 1)


def down(x):
    high, low = split(x)
    return jnp.concatenate([high, low, high], 0)


def call(body, shapes, specs, flops, name, scratch=()):
    return pl.pallas_call(
        body,
        out_shape=shapes,
        in_specs=specs,
        out_specs=jax.tree.map(lambda _: VMEM, shapes),
        scratch_shapes=scratch,
        compiler_params=pltpu.CompilerParams(vmem_limit_bytes=8 << 20),
        cost_estimate=pl.CostEstimate(flops=1, bytes_accessed=1, transcendentals=0),
        name=name,
    )


def begin_kernel(d, own, core, right, e_out, rt_out):
    q = lax.axis_index("col")
    nodes, depth, _ = own.shape
    for n in range(nodes):
        e_out[n] = dot(d[n, :, band(q, depth)], own[n]) + dot(d[n, :, band(q ^ 1, depth)], core[n])
        rt_out[n] = right[n].T


def eliminate_kernel(n, e, d, chip, cross, rt, s_out):
    q = lax.axis_index("col")
    depth = chip.shape[0]
    elim = e[n] + dot(d[n, :, band(q ^ 2, depth)], chip[...]) + dot(d[n, :, band(q ^ 3, depth)], cross[...])
    s_out[...] = dot(rt[n], elim.astype(BF16))


def couple_kernel(blocks, c_own, c_core, m_out, mt_out, cm_out, m, sib, c_all):
    q = lax.axis_index("col")
    nodes, part, width = c_own.shape
    for n in range(nodes):
        for k in range(4):
            m[band(q ^ k, part), :] = blocks[k, 0, n]
            sib[band(q ^ k, part), :] = blocks[k, 1, n]
        c_all[band(q & 1, part), :] = c_own[n]
        c_all[band(1 - (q & 1), part), :] = c_core[n]
        cm_out[n] = dot(across(c_all[...]), down(sib[...]))
        m_out[n] = down(m[...])
        m[...] = m[...].T
        mt_out[n] = across(jnp.concatenate([m[band(q, part), :], m[band(q ^ 2, part), :]], 0))


def merge_kernel(n, ranks, s_own, s_core, m, mt, cm, own_out, send_out, t_all):
    q = lax.axis_index("col")
    rank = ranks[n]
    part = cm.shape[1] // 2
    width = m.shape[2]
    row = lax.broadcasted_iota(jnp.int32, (width, width), 0)
    col = lax.broadcasted_iota(jnp.int32, (width, width), 1)
    s = jnp.where((row < rank) & (col < rank), s_own[...] + s_core[...], 0.0)
    t_all[...] = dot(across(s), m[n])
    t_all[band(q >> 1, 2 * part), :] += cm[n]
    high, low = split(t_all[...])
    p = dot(mt[n], jnp.concatenate([high, low, high], 0))
    own_out[0] = t_all[band(q, part), :]
    own_out[1] = p[:part]
    send_out[0] = t_all[band(q ^ 2, part), :].astype(BF16)
    send_out[1] = p[part:].astype(BF16)


def shards(diagonal_inverses, column_basis, row_basis, transfer, coupling, ranks):
    nodes, part, width = transfer.shape
    depth = column_basis.shape[1]
    q = lax.axis_index("col").astype(jnp.int32)
    shape = jax.ShapeDtypeStruct

    first = column_basis[0]
    chip_left = [to_chip(first)]
    transfer, ranks_late = lax.optimization_barrier((transfer, ranks, first))[:2]
    rows = q * part + jnp.arange(part, dtype=jnp.int32)
    live = (rows[None, :] < ranks_late[:, None])[:, :, None]
    m_own = jnp.where(live, transfer * SCALE, 0.0).astype(F16)
    m_chip = to_chip(m_own)
    rest = after(column_basis, m_own)
    pieces = lax.optimization_barrier(tuple(rest[n] for n in range(1, nodes)))
    chip_left += [to_chip(piece) for piece in pieces]
    own_left = after(column_basis, *pieces)
    core_left = to_core(column_basis)
    c_core = to_core(coupling)

    e, rt = call(
        begin_kernel,
        [shape((nodes, depth, width), F32), shape((nodes, width, depth), BF16)],
        [VMEM] * 4,
        2 * nodes * depth * 2 * depth * width,
        "begin",
    )(diagonal_inverses, own_left, core_left, row_basis)
    left0, m_chip = lax.optimization_barrier((chip_left[0], m_chip, e))[:2]

    def eliminate(n, chip, cross):
        return call(
            functools.partial(eliminate_kernel, n),
            shape((width, width), F32),
            [VMEM] * 5,
            2 * depth * 2 * depth * width,
            f"eliminate{n}",
        )(e, diagonal_inverses, chip, cross, rt)

    def merge(n, s, s_core):
        return call(
            functools.partial(merge_kernel, n),
            [shape((2, part, width), F32), shape((2, part, width), BF16)],
            [SMEM] + [VMEM] * 5,
            12 * width**3,
            f"merge{n}",
            [pltpu.VMEM((width, width), F32)],
        )(ranks, s, s_core, m, mt, cm)

    s0 = eliminate(0, left0, to_core(left0))
    s0_core = to_core(s0)

    m_pair = jnp.stack([m_own, m_chip])
    m_sib = to_sibling(m_pair)
    m_mine = jnp.stack([m_pair, m_sib], 1)
    m_core = to_core(m_mine)

    left1 = after(chip_left[1], s0)
    s1 = eliminate(1, left1, to_core(left1))
    s1_core = to_core(s1)

    blocks = jnp.stack([m_mine[0], m_core[0], m_mine[1], m_core[1]]).astype(F32) * (1 / SCALE)
    m, mt, cm = call(
        couple_kernel,
        [
            shape((nodes, 3 * width, width), BF16),
            shape((nodes, 2 * part, 3 * width), BF16),
            shape((nodes, 2 * part, width), F32),
        ],
        [VMEM] * 3,
        6 * nodes * 2 * part * width * width,
        "couple",
        [pltpu.VMEM((width, width), F32), pltpu.VMEM((width, width), F32), pltpu.VMEM((2 * part, width), F32)],
    )(blocks, coupling, c_core)

    own0, send0 = merge(0, s0, s0_core)
    left2 = after(chip_left[2], own0)
    s1, s1_core = lax.optimization_barrier((s1, s1_core, left2))[:2]
    own1, send1 = merge(1, s1, s1_core)
    s2 = eliminate(2, left2, to_core(left2))
    got0 = to_chip(jnp.stack([send0, send1]))
    own2, send2 = merge(2, s2, to_core(s2))
    got2 = to_chip(send2)
    p01 = jnp.stack([own0[1], own1[1]]) + got0[:, 1].astype(F32)
    p01_sib = to_sibling(p01)
    p2 = own2[1] + got2[1].astype(F32)
    p2_sib = to_sibling(p2)
    merged = jnp.stack([own0[0], own1[0], own2[0]]) + jnp.concatenate([got0[:, 0], got2[:1]]).astype(F32)
    parent = jnp.concatenate([p01 + p01_sib, (p2 + p2_sib)[None]])
    return merged, parent


def solution(mesh):
    block = P("row", "col", None)
    return jax.shard_map(
        shards,
        mesh=mesh,
        in_specs=(block, block, block, block, block, P("row")),
        out_specs=(block, block),
        check_vma=False,
    )
```

```python
import functools

import jax
import jax.numpy as jnp
from jax import lax
from jax.experimental import pallas as pl
from jax.experimental.pallas import tpu as pltpu
from jax.sharding import PartitionSpec as P

BIT = 2
F32 = jnp.float32
BF16 = jnp.bfloat16
F16 = jnp.float16
SCALE = 2.0**17
CORE = [(0, 1), (1, 0), (2, 3), (3, 2)]
CHIP = [(0, 2), (2, 0), (1, 3), (3, 1)]
VMEM = pl.BlockSpec(memory_space=pltpu.VMEM)
SMEM = pl.BlockSpec(memory_space=pltpu.SMEM)


def to_core(block):
    return lax.ppermute(block, "col", CORE)


def to_chip(block):
    return lax.ppermute(block, "col", CHIP)


def to_sibling(block):
    return lax.ppermute(block, "row", [(n, n ^ 1 << BIT) for n in range(lax.axis_size("row"))])


def after(block, *earlier):
    return lax.optimization_barrier((block, *earlier))[0]


def dot(a, b):
    return lax.dot_general(a, b, (((1,), (0,)), ((), ())), preferred_element_type=F32)


def band(index, size):
    return pl.ds(pl.multiple_of(index * size, size), size)


def split(x):
    high = x.astype(BF16)
    return high, (x - high.astype(F32)).astype(BF16)


def across(x):
    high, low = split(x)
    return jnp.concatenate([high, high, low], 1)


def down(x):
    high, low = split(x)
    return jnp.concatenate([high, low, high], 0)


def call(body, shapes, specs, flops, name, scratch=()):
    return pl.pallas_call(
        body,
        out_shape=shapes,
        in_specs=specs,
        out_specs=jax.tree.map(lambda _: VMEM, shapes),
        scratch_shapes=scratch,
        compiler_params=pltpu.CompilerParams(vmem_limit_bytes=8 << 20),
        cost_estimate=pl.CostEstimate(flops=1, bytes_accessed=1, transcendentals=0),
        name=name,
    )


def begin_kernel(d, own, core, right, e_out, rt_out):
    q = lax.axis_index("col")
    nodes, depth, _ = own.shape
    for n in range(nodes):
        e_out[n] = dot(d[n, :, band(q, depth)], own[n]) + dot(d[n, :, band(q ^ 1, depth)], core[n])
        rt_out[n] = right[n].T


def eliminate_kernel(n, e, d, chip, cross_a, cross_b, rt, s_out):
    q = lax.axis_index("col")
    depth = chip.shape[0]
    cross = jnp.concatenate([cross_a[...], cross_b[...]], 0)
    elim = e[n] + dot(d[n, :, band(q ^ 2, depth)], chip[...]) + dot(d[n, :, band(q ^ 3, depth)], cross)
    s_out[...] = dot(rt[n], elim.astype(BF16))


def couple_kernel(blocks, c_own, c_core, m_out, mt_out, cm_out, m, sib, c_all):
    q = lax.axis_index("col")
    nodes, part, width = c_own.shape
    for n in range(nodes):
        for k in range(4):
            m[band(q ^ k, part), :] = blocks[k, 0, n]
            sib[band(q ^ k, part), :] = blocks[k, 1, n]
        c_all[band(q & 1, part), :] = c_own[n]
        c_all[band(1 - (q & 1), part), :] = c_core[n]
        cm_out[n] = dot(across(c_all[...]), down(sib[...]))
        m_out[n] = down(m[...])
        m[...] = m[...].T
        mt_out[n] = across(jnp.concatenate([m[band(q, part), :], m[band(q ^ 2, part), :]], 0))


def merge_kernel(n, ranks, s_own, s_core, m, mt, cm, own_out, send_out, t_all):
    q = lax.axis_index("col")
    rank = ranks[n]
    part = cm.shape[1] // 2
    width = m.shape[2]
    row = lax.broadcasted_iota(jnp.int32, (width, width), 0)
    col = lax.broadcasted_iota(jnp.int32, (width, width), 1)
    s = jnp.where((row < rank) & (col < rank), s_own[...] + s_core[...], 0.0)
    t_all[...] = dot(across(s), m[n])
    t_all[band(q >> 1, 2 * part), :] += cm[n]
    high, low = split(t_all[...])
    p = dot(mt[n], jnp.concatenate([high, low, high], 0))
    own_out[0] = t_all[band(q, part), :]
    own_out[1] = p[:part]
    send_out[0] = t_all[band(q ^ 2, part), :].astype(BF16)
    send_out[1] = p[part:].astype(BF16)


def shards(diagonal_inverses, column_basis, row_basis, transfer, coupling, ranks):
    nodes, part, width = transfer.shape
    depth = column_basis.shape[1]
    q = lax.axis_index("col").astype(jnp.int32)
    shape = jax.ShapeDtypeStruct

    first = column_basis[0]
    chip_left = [to_chip(first)]
    transfer, ranks_late = lax.optimization_barrier((transfer, ranks, first))[:2]
    rows = q * part + jnp.arange(part, dtype=jnp.int32)
    live = (rows[None, :] < ranks_late[:, None])[:, :, None]
    m_own = jnp.where(live, transfer * SCALE, 0.0).astype(F16)
    m_chip = to_chip(m_own)
    chip_left.append(to_chip(after(column_basis, m_own)[1]))
    core_left = to_core(column_basis)
    c_core = to_core(coupling)

    e, rt = call(
        begin_kernel,
        [shape((nodes, depth, width), F32), shape((nodes, width, depth), BF16)],
        [VMEM] * 4,
        2 * nodes * depth * 2 * depth * width,
        "begin",
    )(diagonal_inverses, column_basis, core_left, row_basis)
    chip_left[0], m_chip, last = lax.optimization_barrier((chip_left[0], m_chip, column_basis, e))[:3]
    chip_left.append(to_chip(last[2]))

    def cross(left):
        half = depth // 2
        return to_core(left[:half]), to_core(left[half:])

    def eliminate(n, chip):
        return call(
            functools.partial(eliminate_kernel, n),
            shape((width, width), F32),
            [VMEM] * 6,
            2 * depth * 2 * depth * width,
            f"eliminate{n}",
        )(e, diagonal_inverses, chip, *cross(chip), rt)

    def merge(n, s, s_core):
        return call(
            functools.partial(merge_kernel, n),
            [shape((2, part, width), F32), shape((2, part, width), BF16)],
            [SMEM] + [VMEM] * 5,
            12 * width**3,
            f"merge{n}",
            [pltpu.VMEM((width, width), F32)],
        )(ranks, s, s_core, m, mt, cm)

    s0 = eliminate(0, chip_left[0])
    s1 = eliminate(1, after(chip_left[1], s0))
    s0_core, s1_core = to_core(s0), to_core(s1)

    sib_own, sib_chip = to_sibling(m_own), to_sibling(m_chip)
    pieces = [m_own, sib_own, to_core(m_own), to_core(sib_own), m_chip, sib_chip, to_core(m_chip), to_core(sib_chip)]
    blocks = (jnp.stack(pieces).astype(F32) * (1 / SCALE)).reshape((4, 2) + m_own.shape)
    m, mt, cm = call(
        couple_kernel,
        [
            shape((nodes, 3 * width, width), BF16),
            shape((nodes, 2 * part, 3 * width), BF16),
            shape((nodes, 2 * part, width), F32),
        ],
        [VMEM] * 3,
        6 * nodes * 2 * part * width * width,
        "couple",
        [pltpu.VMEM((width, width), F32), pltpu.VMEM((width, width), F32), pltpu.VMEM((2 * part, width), F32)],
    )(blocks, coupling, c_core)

    left2 = after(chip_left[2], s0, s1)
    s2 = eliminate(2, left2)
    own0, send0 = merge(0, s0, s0_core)
    own1, send1 = merge(1, s1, s1_core)
    got0 = to_chip(jnp.stack([send0, send1]))
    own2, send2 = merge(2, s2, to_core(s2))
    got2 = to_chip(send2)
    got0 = after(got0, own2)
    p01 = jnp.stack([own0[1], own1[1]]) + got0[:, 1].astype(F32)
    p01_sib = to_sibling(p01)
    p2 = own2[1] + got2[1].astype(F32)
    p2_sib = to_sibling(p2)
    merged = jnp.stack([own0[0], own1[0], own2[0]]) + jnp.concatenate([got0[:, 0], got2[:1]]).astype(F32)
    parent = jnp.concatenate([p01 + p01_sib, (p2 + p2_sib)[None]])
    return merged, parent


def solution(mesh):
    block = P("row", "col", None)
    return jax.shard_map(
        shards,
        mesh=mesh,
        in_specs=(block, block, block, block, block, P("row")),
        out_specs=(block, block),
        check_vma=False,
    )
```

```python
import functools

import jax
import jax.numpy as jnp
from jax import lax
from jax.experimental import pallas as pl
from jax.experimental.pallas import tpu as pltpu
from jax.sharding import PartitionSpec as P

BIT = 2
F32 = jnp.float32
BF16 = jnp.bfloat16
F16 = jnp.float16
SCALE = 2.0**17
CORE = [(0, 1), (1, 0), (2, 3), (3, 2)]
CHIP = [(0, 2), (2, 0), (1, 3), (3, 1)]
VMEM = pl.BlockSpec(memory_space=pltpu.VMEM)
SMEM = pl.BlockSpec(memory_space=pltpu.SMEM)


def to_core(block):
    return lax.ppermute(block, "col", CORE)


def to_chip(block):
    return lax.ppermute(block, "col", CHIP)


def to_sibling(block):
    return lax.ppermute(block, "row", [(n, n ^ 1 << BIT) for n in range(lax.axis_size("row"))])


def after(block, *earlier):
    return lax.optimization_barrier((block, *earlier))[0]


def dot(a, b):
    return lax.dot_general(a, b, (((1,), (0,)), ((), ())), preferred_element_type=F32)


def band(index, size):
    return pl.ds(pl.multiple_of(index * size, size), size)


def split(x):
    high = x.astype(BF16)
    return high, (x - high.astype(F32)).astype(BF16)


def across(x):
    high, low = split(x)
    return jnp.concatenate([high, high, low], 1)


def down(x):
    high, low = split(x)
    return jnp.concatenate([high, low, high], 0)


def call(body, shapes, specs, name, scratch=(), mib=8):
    return pl.pallas_call(
        body,
        out_shape=shapes,
        in_specs=specs,
        out_specs=jax.tree.map(lambda _: VMEM, shapes),
        scratch_shapes=scratch,
        compiler_params=pltpu.CompilerParams(vmem_limit_bytes=mib << 20),
        cost_estimate=pl.CostEstimate(flops=1, bytes_accessed=1, transcendentals=0),
        name=name,
    )


def begin_kernel(d, own, core, right, e_out, rt_out, far_out, near, sem):
    q = lax.axis_index("col")
    nodes, depth, _ = own.shape
    copies = [
        pltpu.make_async_copy(d.at[n, :, band(q >> 1, 2 * depth)], near.at[n], sem.at[0, n]) for n in range(nodes)
    ]
    others = [
        pltpu.make_async_copy(d.at[n, :, band(1 - (q >> 1), 2 * depth)], far_out.at[n], sem.at[1, n]) for n in range(nodes)
    ]
    for copy in copies + others:
        copy.start()
    for n in range(nodes):
        rt_out[n] = right[n].T
    for n in range(nodes):
        copies[n].wait()
        e_out[n] = dot(near[n, :, band(q & 1, depth)], own[n]) + dot(near[n, :, band(1 - (q & 1), depth)], core[n])
    for copy in others:
        copy.wait()


def eliminate_kernel(n, e, d, chip, cross_a, cross_b, rt, s_out):
    q = lax.axis_index("col")
    depth = chip.shape[0]
    cross = jnp.concatenate([cross_a[...], cross_b[...]], 0)
    elim = e[n] + dot(d[n, :, band(q & 1, depth)], chip[...]) + dot(d[n, :, band(1 - (q & 1), depth)], cross)
    s_out[...] = dot(rt[n], elim.astype(BF16))


def couple_kernel(blocks, c_own, c_core, m_out, mt_out, cm_out, m, sib, c_all):
    q = lax.axis_index("col")
    nodes, part, width = c_own.shape
    for n in range(nodes):
        for k in range(4):
            m[band(q ^ k, part), :] = blocks[k, 0, n]
            sib[band(q ^ k, part), :] = blocks[k, 1, n]
        c_all[band(q & 1, part), :] = c_own[n]
        c_all[band(1 - (q & 1), part), :] = c_core[n]
        cm_out[n] = dot(across(c_all[...]), down(sib[...]))
        m_out[n] = down(m[...])
        m[...] = m[...].T
        mt_out[n] = across(jnp.concatenate([m[band(q, part), :], m[band(q ^ 2, part), :]], 0))


def merge_kernel(n, ranks, s_own, s_core, m, mt, cm, own_out, send_out, t_all):
    q = lax.axis_index("col")
    rank = ranks[n]
    part = cm.shape[1] // 2
    width = m.shape[2]
    row = lax.broadcasted_iota(jnp.int32, (width, width), 0)
    col = lax.broadcasted_iota(jnp.int32, (width, width), 1)
    s = jnp.where((row < rank) & (col < rank), s_own[...] + s_core[...], 0.0)
    t_all[...] = dot(across(s), m[n])
    t_all[band(q >> 1, 2 * part), :] += cm[n]
    high, low = split(t_all[...])
    p = dot(mt[n], jnp.concatenate([high, low, high], 0))
    own_out[0] = t_all[band(q, part), :]
    own_out[1] = p[:part]
    send_out[0] = t_all[band(q ^ 2, part), :].astype(BF16)
    send_out[1] = p[part:].astype(BF16)


def shards(diagonal_inverses, column_basis, row_basis, transfer, coupling, ranks):
    nodes, part, width = transfer.shape
    depth = column_basis.shape[1]
    q = lax.axis_index("col").astype(jnp.int32)
    shape = jax.ShapeDtypeStruct

    first = column_basis[0]
    chip_left = [to_chip(first)]
    transfer, ranks_late = lax.optimization_barrier((transfer, ranks, first))[:2]
    rows = q * part + jnp.arange(part, dtype=jnp.int32)
    live = (rows[None, :] < ranks_late[:, None])[:, :, None]
    m_own = jnp.where(live, transfer * SCALE, 0.0).astype(F16)
    m_chip, sib_own = to_chip(m_own), to_sibling(m_own)
    chip_left.append(to_chip(after(column_basis, m_own)[1]))
    core_left = to_core(column_basis)
    c_core = to_core(coupling)

    e, rt, d = call(
        begin_kernel,
        [shape((nodes, depth, width), F32), shape((nodes, width, depth), BF16), shape((nodes, depth, 2 * depth), BF16)],
        [pl.BlockSpec(memory_space=pltpu.HBM), VMEM, VMEM, VMEM],
        "begin",
        [pltpu.VMEM((nodes, depth, 2 * depth), BF16), pltpu.SemaphoreType.DMA((2, nodes))],
        45,
    )(diagonal_inverses, column_basis, core_left, row_basis)
    chip_left[0], m_chip, sib_own, last = lax.optimization_barrier((chip_left[0], m_chip, sib_own, column_basis, e))[:4]
    chip_left.append(to_chip(last[2]))

    def cross(left):
        half = depth // 2
        return to_core(left[:half]), to_core(left[half:])

    def eliminate(n, chip, *earlier):
        return call(
            functools.partial(eliminate_kernel, n),
            shape((width, width), F32),
            [VMEM] * 6,
            f"eliminate{n}",
        )(after(e, *earlier), d, chip, *cross(chip), rt)

    def merge(n, s, s_core):
        return call(
            functools.partial(merge_kernel, n),
            [shape((2, part, width), F32), shape((2, part, width), BF16)],
            [SMEM] + [VMEM] * 5,
            f"merge{n}",
            [pltpu.VMEM((width, width), F32)],
        )(ranks, s, s_core, m, mt, cm)

    s0 = eliminate(0, chip_left[0])
    s1 = eliminate(1, after(chip_left[1], s0))
    s0_core, s1_core = to_core(s0), to_core(s1)

    sib_chip = after(to_sibling(m_chip), s0)
    pieces = [m_own, sib_own, to_core(m_own), to_core(sib_own), m_chip, sib_chip, to_core(m_chip), to_core(sib_chip)]
    blocks = (jnp.stack(pieces).astype(F32) * (1 / SCALE)).reshape((4, 2) + m_own.shape)
    m, mt, cm = call(
        couple_kernel,
        [
            shape((nodes, 3 * width, width), BF16),
            shape((nodes, 2 * part, 3 * width), BF16),
            shape((nodes, 2 * part, width), F32),
        ],
        [VMEM] * 3,
        "couple",
        [pltpu.VMEM((width, width), F32), pltpu.VMEM((width, width), F32), pltpu.VMEM((2 * part, width), F32)],
    )(blocks, coupling, c_core)

    own0, send0 = merge(0, s0, s0_core)
    left2 = after(chip_left[2], s1, own0)
    own1, send1 = merge(1, s1, s1_core)
    s2 = eliminate(2, left2, own1)
    got = to_chip(jnp.stack([send0, send1]))
    own2, send2 = merge(2, s2, to_core(s2))
    got2 = to_chip(send2)
    got = after(got, got2)
    own = jnp.stack([own0, own1, own2]) + jnp.concatenate([got, got2[None]]).astype(F32)
    merged, share = own[:, 0], own[:, 1]
    parent = share + to_sibling(share.astype(BF16)).astype(F32)
    return merged, parent


def solution(mesh):
    block = P("row", "col", None)
    return jax.shard_map(
        shards,
        mesh=mesh,
        in_specs=(block, block, block, block, block, P("row")),
        out_specs=(block, block),
        check_vma=False,
    )
```

```python
import functools

import jax
import jax.numpy as jnp
from jax import lax
from jax.experimental import pallas as pl
from jax.experimental.pallas import tpu as pltpu
from jax.sharding import PartitionSpec as P

BIT = 2
F32 = jnp.float32
BF16 = jnp.bfloat16
F16 = jnp.float16
SCALE = 2.0**17
CORE = [(0, 1), (1, 0), (2, 3), (3, 2)]
CHIP = [(0, 2), (2, 0), (1, 3), (3, 1)]
VMEM = pl.BlockSpec(memory_space=pltpu.VMEM)
SMEM = pl.BlockSpec(memory_space=pltpu.SMEM)


def to_core(block):
    return lax.ppermute(block, "col", CORE)


def to_chip(block):
    return lax.ppermute(block, "col", CHIP)


def to_sibling(block):
    return lax.ppermute(block, "row", [(n, n ^ 1 << BIT) for n in range(lax.axis_size("row"))])


def after(block, *earlier):
    return lax.optimization_barrier((block, *earlier))[0]


def dot(a, b):
    return lax.dot_general(a, b, (((1,), (0,)), ((), ())), preferred_element_type=F32)


def band(index, size):
    return pl.ds(pl.multiple_of(index * size, size), size)


def split(x):
    high = x.astype(BF16)
    return high, (x - high.astype(F32)).astype(BF16)


def across(x):
    high, low = split(x)
    return jnp.concatenate([high, high, low], 1)


def down(x):
    high, low = split(x)
    return jnp.concatenate([high, low, high], 0)


def call(body, shapes, specs, name, scratch=(), mib=8):
    return pl.pallas_call(
        body,
        out_shape=shapes,
        in_specs=specs,
        out_specs=jax.tree.map(lambda _: VMEM, shapes),
        scratch_shapes=scratch,
        compiler_params=pltpu.CompilerParams(vmem_limit_bytes=mib << 20),
        cost_estimate=pl.CostEstimate(flops=1, bytes_accessed=1, transcendentals=0),
        name=name,
    )


def begin_kernel(d, own, core, right, e_out, rt_out, far_out, near, sem):
    q = lax.axis_index("col")
    nodes, depth, _ = own.shape
    copies = [
        pltpu.make_async_copy(d.at[n, :, band(q >> 1, 2 * depth)], near.at[n], sem.at[0, n]) for n in range(nodes)
    ]
    others = [
        pltpu.make_async_copy(d.at[n, :, band(1 - (q >> 1), 2 * depth)], far_out.at[n], sem.at[1, n]) for n in range(nodes)
    ]
    for copy in copies + others:
        copy.start()
    for n in range(nodes):
        rt_out[n] = right[n].T
    for n in range(nodes):
        copies[n].wait()
        e_out[n] = dot(near[n, :, band(q & 1, depth)], own[n]) + dot(near[n, :, band(1 - (q & 1), depth)], core[n])
    for copy in others:
        copy.wait()


def eliminate_kernel(n, e, d, chip, cross_a, cross_b, rt, s_out):
    q = lax.axis_index("col")
    depth = chip.shape[0]
    cross = jnp.concatenate([cross_a[...], cross_b[...]], 0)
    elim = e[n] + dot(d[n, :, band(q & 1, depth)], chip[...]) + dot(d[n, :, band(1 - (q & 1), depth)], cross)
    s_out[...] = dot(rt[n], elim.astype(BF16))


def couple_kernel(blocks, c_own, c_core, m_out, mt_out, cm_out, m, sib, c_all):
    q = lax.axis_index("col")
    nodes, part, width = c_own.shape
    for n in range(nodes):
        for k in range(4):
            m[band(q ^ k, part), :] = blocks[k, 0, n]
            sib[band(q ^ k, part), :] = blocks[k, 1, n]
        c_all[band(q & 1, part), :] = c_own[n]
        c_all[band(1 - (q & 1), part), :] = c_core[n]
        cm_out[n] = dot(across(c_all[...]), down(sib[...]))
        m_out[n] = down(m[...])
        m[...] = m[...].T
        mt_out[n] = across(jnp.concatenate([m[band(q, part), :], m[band(q ^ 2, part), :]], 0))


def merge_kernel(n, ranks, s_own, s_core, m, mt, cm, own_out, send_out, t_all):
    q = lax.axis_index("col")
    rank = ranks[n]
    part = cm.shape[1] // 2
    width = m.shape[2]
    row = lax.broadcasted_iota(jnp.int32, (width, width), 0)
    col = lax.broadcasted_iota(jnp.int32, (width, width), 1)
    s = jnp.where((row < rank) & (col < rank), s_own[...] + s_core[...], 0.0)
    t_all[...] = dot(across(s), m[n])
    t_all[band(q >> 1, 2 * part), :] += cm[n]
    high, low = split(t_all[...])
    p = dot(mt[n], jnp.concatenate([high, low, high], 0))
    own_out[0] = t_all[band(q, part), :]
    own_out[1] = p[:part]
    send_out[0] = t_all[band(q ^ 2, part), :].astype(BF16)
    send_out[1] = p[part:].astype(BF16)


def shards(diagonal_inverses, column_basis, row_basis, transfer, coupling, ranks):
    nodes, part, width = transfer.shape
    depth = column_basis.shape[1]
    q = lax.axis_index("col").astype(jnp.int32)
    shape = jax.ShapeDtypeStruct

    first = column_basis[0]
    chip_left = [to_chip(first)]
    transfer, ranks_late = lax.optimization_barrier((transfer, ranks, first))[:2]
    rows = lax.broadcasted_iota(jnp.int32, transfer.shape, 1) + q * part
    live = rows < ranks_late[:, None, None]
    m_own = jnp.where(live, transfer * SCALE, 0.0).astype(F16)
    m_chip, sib_own = to_chip(m_own), to_sibling(m_own)
    chip_left.append(to_chip(after(column_basis, m_own)[1]))
    core_left = to_core(column_basis)
    c_core = to_core(coupling)

    e, rt, d = call(
        begin_kernel,
        [shape((nodes, depth, width), F32), shape((nodes, width, depth), BF16), shape((nodes, depth, 2 * depth), BF16)],
        [pl.BlockSpec(memory_space=pltpu.HBM), VMEM, VMEM, VMEM],
        "begin",
        [pltpu.VMEM((nodes, depth, 2 * depth), BF16), pltpu.SemaphoreType.DMA((2, nodes))],
        45,
    )(diagonal_inverses, column_basis, core_left, row_basis)
    chip_left[0], sib_own, last = lax.optimization_barrier((chip_left[0], sib_own, column_basis, e))[:3]
    chip_left.append(to_chip(last[2]))

    def cross(left):
        half = depth // 2
        return to_core(left[:half]), to_core(left[half:])

    def eliminate(n, chip, *earlier):
        return call(
            functools.partial(eliminate_kernel, n),
            shape((width, width), F32),
            [VMEM] * 6,
            f"eliminate{n}",
        )(after(e, *earlier), d, chip, *cross(chip), rt)

    def merge(n, s, s_core):
        return call(
            functools.partial(merge_kernel, n),
            [shape((2, part, width), F32), shape((2, part, width), BF16)],
            [SMEM] + [VMEM] * 5,
            f"merge{n}",
            [pltpu.VMEM((width, width), F32)],
        )(ranks, s, s_core, m, mt, cm)

    s0 = eliminate(0, chip_left[0])
    s1 = eliminate(1, after(chip_left[1], s0))
    s0_core, s1_core = to_core(s0), to_core(s1)

    sib_chip = after(to_sibling(m_chip), s0)
    pieces = [m_own, sib_own, to_core(m_own), to_core(sib_own), m_chip, sib_chip, to_core(m_chip), to_core(sib_chip)]
    blocks = (jnp.stack(pieces).astype(F32) * (1 / SCALE)).reshape((4, 2) + m_own.shape)
    m, mt, cm = call(
        couple_kernel,
        [
            shape((nodes, 3 * width, width), BF16),
            shape((nodes, 2 * part, 3 * width), BF16),
            shape((nodes, 2 * part, width), F32),
        ],
        [VMEM] * 3,
        "couple",
        [pltpu.VMEM((width, width), F32), pltpu.VMEM((width, width), F32), pltpu.VMEM((2 * part, width), F32)],
    )(blocks, coupling, c_core)

    own0, send0 = merge(0, s0, s0_core)
    left2 = after(chip_left[2], s1, own0)
    own1, send1 = merge(1, s1, s1_core)
    s2 = eliminate(2, left2, own1)
    got = to_chip(jnp.stack([send0, send1]))
    own2, send2 = merge(2, s2, to_core(s2))
    got2 = to_chip(send2)
    got = after(got, got2)
    own = jnp.stack([own0, own1, own2]) + jnp.concatenate([got, got2[None]]).astype(F32)
    merged, share = own[:, 0], own[:, 1]
    parent = share + to_sibling(share.astype(BF16)).astype(F32)
    return merged, parent


def solution(mesh):
    block = P("row", "col", None)
    return jax.shard_map(
        shards,
        mesh=mesh,
        in_specs=(block, block, block, block, block, P("row")),
        out_specs=(block, block),
        check_vma=False,
    )
```

```python
import functools

import jax
import jax.numpy as jnp
from jax import lax
from jax.experimental import pallas as pl
from jax.experimental.pallas import tpu as pltpu
from jax.sharding import PartitionSpec as P

BIT = 2
F32 = jnp.float32
BF16 = jnp.bfloat16
F16 = jnp.float16
SCALE = 2.0**17
CORE = [(0, 1), (1, 0), (2, 3), (3, 2)]
CHIP = [(0, 2), (2, 0), (1, 3), (3, 1)]
VMEM = pl.BlockSpec(memory_space=pltpu.VMEM)
SMEM = pl.BlockSpec(memory_space=pltpu.SMEM)


def to_core(block):
    return lax.ppermute(block, "col", CORE)


def to_chip(block):
    return lax.ppermute(block, "col", CHIP)


def to_sibling(block):
    return lax.ppermute(block, "row", [(n, n ^ 1 << BIT) for n in range(lax.axis_size("row"))])


def after(block, *earlier):
    return lax.optimization_barrier((block, *earlier))[0]


def dot(a, b):
    return lax.dot_general(a, b, (((1,), (0,)), ((), ())), preferred_element_type=F32)


def band(index, size):
    return pl.ds(pl.multiple_of(index * size, size), size)


def split(x):
    high = x.astype(BF16)
    return high, (x - high.astype(F32)).astype(BF16)


def across(x):
    high, low = split(x)
    return jnp.concatenate([high, high, low], 1)


def down(x):
    high, low = split(x)
    return jnp.concatenate([high, low, high], 0)


def call(body, shapes, specs, name, scratch=(), mib=8):
    return pl.pallas_call(
        body,
        out_shape=shapes,
        in_specs=specs,
        out_specs=jax.tree.map(lambda _: VMEM, shapes),
        scratch_shapes=scratch,
        compiler_params=pltpu.CompilerParams(vmem_limit_bytes=mib << 20),
        cost_estimate=pl.CostEstimate(flops=1, bytes_accessed=1, transcendentals=0),
        name=name,
    )


def begin_kernel(d, own, core, right, e_out, rt_out, far_out, near, sem):
    q = lax.axis_index("col")
    nodes, depth, _ = own.shape
    copies = [
        pltpu.make_async_copy(d.at[n, :, band(q >> 1, 2 * depth)], near.at[n], sem.at[0, n]) for n in range(nodes)
    ]
    others = [
        pltpu.make_async_copy(d.at[n, :, band(1 - (q >> 1), 2 * depth)], far_out.at[n], sem.at[1, n]) for n in range(nodes)
    ]
    for copy in copies + others:
        copy.start()
    for n in range(nodes):
        rt_out[n] = right[n].T
    for n in range(nodes):
        copies[n].wait()
        e_out[n] = dot(near[n, :, band(q & 1, depth)], own[n]) + dot(near[n, :, band(1 - (q & 1), depth)], core[n])
    for copy in others:
        copy.wait()


def eliminate_kernel(n, e, d, chip, cross, rt, s_out):
    q = lax.axis_index("col")
    depth = chip.shape[0]
    elim = e[n] + dot(d[n, :, band(q & 1, depth)], chip[...]) + dot(d[n, :, band(1 - (q & 1), depth)], cross[...])
    s_out[...] = dot(rt[n], elim.astype(BF16))


def couple_kernel(blocks, c_own, c_core, m_out, mt_out, cm_out, m, sib, c_all):
    q = lax.axis_index("col")
    nodes, part, width = c_own.shape
    for n in range(nodes):
        for k in range(4):
            m[band(q ^ k, part), :] = blocks[k, 0, n]
            sib[band(q ^ k, part), :] = blocks[k, 1, n]
        c_all[band(q & 1, part), :] = c_own[n]
        c_all[band(1 - (q & 1), part), :] = c_core[n]
        cm_out[n] = dot(across(c_all[...]), down(sib[...]))
        m_out[n] = down(m[...])
        m[...] = m[...].T
        mt_out[n] = across(jnp.concatenate([m[band(q, part), :], m[band(q ^ 2, part), :]], 0))


def merge_kernel(n, ranks, s_own, s_core, m, mt, cm, own_out, send_out, t_all):
    q = lax.axis_index("col")
    rank = ranks[n]
    part = cm.shape[1] // 2
    width = m.shape[2]
    row = lax.broadcasted_iota(jnp.int32, (width, width), 0)
    col = lax.broadcasted_iota(jnp.int32, (width, width), 1)
    s = jnp.where((row < rank) & (col < rank), s_own[...] + s_core[...], 0.0)
    t_all[...] = dot(across(s), m[n])
    t_all[band(q >> 1, 2 * part), :] += cm[n]
    high, low = split(t_all[...])
    p = dot(mt[n], jnp.concatenate([high, low, high], 0))
    own_out[0] = t_all[band(q, part), :]
    own_out[1] = p[:part]
    send_out[0] = t_all[band(q ^ 2, part), :].astype(BF16)
    send_out[1] = p[part:].astype(BF16)


def shards(diagonal_inverses, column_basis, row_basis, transfer, coupling, ranks):
    nodes, part, width = transfer.shape
    depth = column_basis.shape[1]
    q = lax.axis_index("col").astype(jnp.int32)
    shape = jax.ShapeDtypeStruct

    first = column_basis[0]
    chip_left = [to_chip(first)]
    transfer, ranks_late = lax.optimization_barrier((transfer, ranks, first))[:2]
    rows = lax.broadcasted_iota(jnp.int32, transfer.shape, 1) + q * part
    live = rows < ranks_late[:, None, None]
    m_own = jnp.where(live, transfer * SCALE, 0.0).astype(F16)
    m_chip, sib_own = to_chip(m_own), to_sibling(m_own)
    chip_left.append(to_chip(after(column_basis, m_own)[1]))
    core_left = to_core(column_basis)
    c_core = to_core(coupling)

    e, rt, d = call(
        begin_kernel,
        [shape((nodes, depth, width), F32), shape((nodes, width, depth), BF16), shape((nodes, depth, 2 * depth), BF16)],
        [pl.BlockSpec(memory_space=pltpu.HBM), VMEM, VMEM, VMEM],
        "begin",
        [pltpu.VMEM((nodes, depth, 2 * depth), BF16), pltpu.SemaphoreType.DMA((2, nodes))],
        45,
    )(diagonal_inverses, column_basis, core_left, row_basis)
    chip_left[0], sib_own, last = lax.optimization_barrier((chip_left[0], sib_own, column_basis, e))[:3]
    chip_left.append(to_chip(last[2]))

    def cross(left):
        return (to_core(left),)

    def eliminate(n, chip, *earlier):
        return call(
            functools.partial(eliminate_kernel, n),
            shape((width, width), F32),
            [VMEM] * 5,
            f"eliminate{n}",
        )(after(e, *earlier), d, chip, *cross(chip), rt)

    def merge(n, s, s_core):
        return call(
            functools.partial(merge_kernel, n),
            [shape((2, part, width), F32), shape((2, part, width), BF16)],
            [SMEM] + [VMEM] * 5,
            f"merge{n}",
            [pltpu.VMEM((width, width), F32)],
        )(ranks, s, s_core, m, mt, cm)

    s0 = eliminate(0, chip_left[0])
    s1 = eliminate(1, after(chip_left[1], s0))
    s0_core, s1_core = to_core(s0), to_core(s1)

    sib_chip = after(to_sibling(m_chip), s0)
    pieces = [m_own, sib_own, to_core(m_own), to_core(sib_own), m_chip, sib_chip, to_core(m_chip), to_core(sib_chip)]
    blocks = (jnp.stack(pieces).astype(F32) * (1 / SCALE)).reshape((4, 2) + m_own.shape)
    m, mt, cm = call(
        couple_kernel,
        [
            shape((nodes, 3 * width, width), BF16),
            shape((nodes, 2 * part, 3 * width), BF16),
            shape((nodes, 2 * part, width), F32),
        ],
        [VMEM] * 3,
        "couple",
        [pltpu.VMEM((width, width), F32), pltpu.VMEM((width, width), F32), pltpu.VMEM((2 * part, width), F32)],
    )(blocks, coupling, c_core)

    own0, send0 = merge(0, s0, s0_core)
    left2 = after(chip_left[2], s1, own0)
    own1, send1 = merge(1, s1, s1_core)
    s2 = eliminate(2, left2, own1)
    got = to_chip(jnp.stack([send0, send1]))
    own2, send2 = merge(2, s2, to_core(s2))
    got2 = to_chip(send2)
    got = after(got, got2)
    own = jnp.stack([own0, own1, own2]) + jnp.concatenate([got, got2[None]]).astype(F32)
    merged, share = own[:, 0], own[:, 1]
    parent = share + to_sibling(share.astype(BF16)).astype(F32)
    return merged, parent


def solution(mesh):
    block = P("row", "col", None)
    return jax.shard_map(
        shards,
        mesh=mesh,
        in_specs=(block, block, block, block, block, P("row")),
        out_specs=(block, block),
        check_vma=False,
    )
```
